256 devices in a mesh: replica: 32 (over z_lo, x, core), shard: 8 (over z_hi, y).
Axes of the slice: x: 4, y: 4, z: 8 (z_hi: 2, z_lo: 4; z = z_hi * 4 + z_lo), core: 2. Of those that a mesh axis runs over, the one named last changes fastest.
Arguments:
- hidden: bfloat16 [65536, 8192], P(('replica', 'shard')), may hold values from -220 to 220
- cotangent: bfloat16 [65536, 1024], P(('replica', 'shard')), may hold values from -6 to 6
- weight: bfloat16 [32, 8192, 1024], P('replica', 'shard'), may hold values from -13 to 13
- gain: float32 [8192], replicated, may hold values from 0.1 to 1.9
- train_logp: float32 [65536], P(('replica', 'shard')), may hold values from -4 to 0
- infer_logp: float32 [65536], P(('replica', 'shard')), may hold values from -4 to 0
- advantage: float32 [65536], P(('replica', 'shard')), may hold values from -6 to 6
- response_mask: int32 [65536], P(('replica', 'shard')), may hold values from 0 to 1, as said below
- step: int32 [1], replicated, may hold values from 0 to 63
Outputs:
- grad_hidden: bfloat16 [65536, 8192], P(('replica', 'shard'))
- new_weight: bfloat16 [32, 8192, 1024], P('replica', 'shard')
The draws below stay inside these ranges and needn't reach their ends.
Inputs may be any that keep to these rules, and one draw needn't show every extreme that they name: `response_mask`: each device's last row is a response token.
All inputs are finite; a program needn't handle non-finite values.
Results may differ from the reference program's by a relative error of at most 0.015.
Values may be sent and summed in bfloat16 or wider, within the bound.
No kernel may reach another device: no remote copies, remote signals or barrier semaphores. Data moves between devices by JAX's collectives and lax.ppermute only.
A program may use at most 128 MiB of HBM per device.

```python
import math
import jax
import jax.numpy as jnp
from jax import lax

D = 8192
TOK_DEV = 256
COLS = 1024
REPLICAS = 32
TOKENS = 65536
N_REPLICA = 32
N_SHARD = 8


def common_direction(key):
    shared_key = jax.random.fold_in(key, 5)
    return jnp.clip(jax.random.normal(shared_key, (D,), jnp.float32), -3.0, 3.0)


def draw_hidden(key, part):
    direction = common_direction(key)
    key = jax.random.fold_in(key, 11)
    base_key, row_key, col_key = jax.random.split(key, 3)
    row_scale = jnp.exp(jax.random.uniform(row_key, (TOKENS, 1), jnp.float32, 0.0, math.log(10.0)))
    col_scale = jnp.exp(jax.random.uniform(col_key, (1, D), jnp.float32, math.log(0.5), math.log(2.0)))
    base = jnp.clip(jax.random.normal(base_key, (TOKENS, D), jnp.float32), -8.0, 8.0)
    return ((base + direction[None, :]) * row_scale * col_scale).astype(jnp.bfloat16)


def draw_weight(key, part):
    direction = common_direction(key)
    key = jax.random.fold_in(key, 31)
    noise_key, beta_key = jax.random.split(key, 2)
    beta = 0.7 * jnp.clip(jax.random.normal(beta_key, (REPLICAS, 1, COLS), jnp.float32), -3.0, 3.0)
    noise = jnp.clip(jax.random.normal(noise_key, (REPLICAS, D, COLS), jnp.float32), -6.0, 6.0)
    return (noise + beta * direction[None, :, None]).astype(jnp.bfloat16)


def draw_response_mask(key, part):
    key = jax.random.fold_in(key, 23)
    position = jnp.arange(TOKENS, dtype=jnp.int32)
    shard_index = position // TOK_DEV % N_SHARD
    threshold = 200 + 600 * shard_index // max(N_SHARD - 1, 1)
    ticket = jax.random.randint(key, (TOKENS,), 0, 1000, dtype=jnp.int32)
    last_row = position % TOK_DEV == TOK_DEV - 1
    return jnp.where((ticket < threshold) | last_row, 1, 0).astype(jnp.int32)


def levels(own_key, shape, shards, smallest, high):
    def one(dim, blocks):
        draws = jax.random.uniform(jax.random.fold_in(jax.random.fold_in(own_key, 6), dim), (blocks,), jnp.float32, smallest / len(shards), high / len(shards))
        return jnp.repeat(jnp.exp(draws), shape[dim] // blocks).reshape((-1,) + (1,) * (len(shape) - dim - 1))

    level = one(*shards[0])
    for cut in shards[1:]:
        level = level * one(*cut)
    return level


def gaussian(own_key, dims, spread, limit, cuts=(), kind=jnp.bfloat16):
    loudness = levels(own_key, dims, cuts, -0.22, 0.18) if cuts else 1.0
    entries = jax.random.normal(own_key, dims, jnp.float32) * spread * loudness
    return jnp.minimum(jnp.maximum(entries, -limit), limit).astype(kind)


def setup_inputs(seed: int = 0) -> dict:
    seeds = jax.random.split(jax.random.key(seed), 10)
    hidden = draw_hidden(jax.random.fold_in(seeds[9], 71), 0)
    cotangent = gaussian(seeds[1], (TOKENS, COLS), 1.0, 6.0, ((0, 256),))
    weight = draw_weight(jax.random.fold_in(seeds[9], 71), 0)
    gain = jnp.clip(1.0 + 0.18 * jax.random.normal(seeds[3], (D,), jnp.float32), 0.1, 1.9)
    train_logp = jnp.clip(-4.0 + 4.0 * jax.random.uniform(seeds[4], (TOKENS,), jnp.float32) ** levels(seeds[4], (TOKENS,), ((0, 256),), -0.2, 0.2), -4.0, 0.0)
    infer_logp = jnp.clip(-4.0 + 4.0 * jax.random.uniform(seeds[5], (TOKENS,), jnp.float32) ** levels(seeds[5], (TOKENS,), ((0, 256),), -0.2, 0.2), -4.0, 0.0)
    advantage = gaussian(seeds[6], (TOKENS,), 1.0, 6.0, ((0, 256),), jnp.float32)
    response_mask = draw_response_mask(jax.random.fold_in(seeds[9], 71), 0)
    step = jax.random.randint(seeds[8], (1,), 0, 64).astype(jnp.int32)
    return {"hidden": hidden, "cotangent": cotangent, "weight": weight, "gain": gain, "train_logp": train_logp, "infer_logp": infer_logp, "advantage": advantage, "response_mask": response_mask, "step": step}


ratio_cap = 2.0
epsilon = 1e-05
learning_rate = 1.0

def replica_step(hidden_rows, cotangent_rows, weight_block, gain, train_rows, infer_rows, advantage_rows, mask_rows):
    multiplier = D ** (-0.5)
    tok_replica = TOK_DEV * N_SHARD
    hidden_f = hidden_rows.astype(jnp.float32)
    inverse = lax.rsqrt(lax.optimization_barrier(jnp.mean(hidden_f * hidden_f, axis=-1, keepdims=True)) + epsilon)
    unit_rows = hidden_f * inverse
    normed = (unit_rows * gain.astype(jnp.float32)).astype(jnp.bfloat16)
    mask_f = mask_rows.astype(jnp.float32)
    responses = jnp.sum(mask_f)
    coefficient = mask_f * jnp.minimum(jnp.exp(train_rows - infer_rows), ratio_cap) * advantage_rows * (tok_replica / responses)
    weighted = (coefficient[:, None] * cotangent_rows.astype(jnp.float32)).astype(jnp.bfloat16)
    grad_normed = (multiplier * jnp.dot(weighted, weight_block.T, preferred_element_type=jnp.float32)).astype(jnp.bfloat16)
    grad_gain = grad_normed.astype(jnp.float32) * gain.astype(jnp.float32)
    grad_hidden = (inverse * (grad_gain - unit_rows * lax.optimization_barrier(jnp.mean(grad_gain * unit_rows, axis=-1, keepdims=True)))).astype(jnp.bfloat16)
    normed_blocks = normed.reshape(N_SHARD, TOK_DEV, D)
    weighted_blocks = weighted.reshape(N_SHARD, TOK_DEV, COLS)

    def accumulate(totals, blocks):
        term = multiplier * jnp.dot(blocks[0].T, blocks[1], preferred_element_type=jnp.float32)
        rounded = lax.optimization_barrier(term.astype(jnp.bfloat16))
        return (totals + rounded.astype(jnp.float32), None)
    weight_grad, unused = lax.scan(accumulate, jnp.zeros((D, COLS), jnp.float32), (normed_blocks, weighted_blocks))
    stored_grad = lax.optimization_barrier(weight_grad.astype(jnp.bfloat16))
    updated = (weight_block.astype(jnp.float32) - learning_rate * stored_grad.astype(jnp.float32)).astype(jnp.bfloat16)
    return (grad_hidden, updated)

def reference(hidden, cotangent, weight, gain, train_logp, infer_logp, advantage, response_mask, step):
    tok_replica = TOK_DEV * N_SHARD
    grouped = (hidden.reshape(N_REPLICA, tok_replica, D), cotangent.reshape(N_REPLICA, tok_replica, COLS), weight, train_logp.reshape(N_REPLICA, tok_replica), infer_logp.reshape(N_REPLICA, tok_replica), advantage.reshape(N_REPLICA, tok_replica), response_mask.reshape(N_REPLICA, tok_replica))

    def one_replica(items):
        return replica_step(items[0], items[1], items[2], gain, items[3], items[4], items[5], items[6])
    grad_hidden, updated = lax.map(one_replica, grouped)
    level = (step[0] % 4).astype(jnp.int32)
    distance = jnp.left_shift(jnp.ones((), jnp.int32), level).astype(jnp.int32)
    partners = jnp.bitwise_xor(jnp.arange(N_REPLICA, dtype=jnp.int32), distance).astype(jnp.int32)
    partner_weights = jnp.take(updated, partners, axis=0)
    new_weight = ((updated.astype(jnp.float32) + partner_weights.astype(jnp.float32)) * 0.5).astype(jnp.bfloat16)
    return (grad_hidden.reshape(TOKENS, D), new_weight)
```

```python
import functools

import jax
import jax.numpy as jnp
from jax import lax
from jax.experimental import pallas as pl
from jax.experimental.pallas import tpu as pltpu
from jax.sharding import PartitionSpec as P

ratio_cap = 2.0
epsilon = 1e-05
learning_rate = 1.0

RING = 4
BLOCK = 1024
TOK = 256
COLS = 1024
PAD = 16
ROWS = 64
STRIP = 16
HALF = BLOCK // 2
CUT = 256
TILE = 256
VMEM = 32 * 1024 * 1024


def around(value, shift):
    pairs = [(s, s // RING * RING + (s + shift) % RING) for s in range(2 * RING)]
    return lax.ppermute(value, "shard", pairs)


def across(value):
    return lax.ppermute(value, "shard", [(s, s ^ RING) for s in range(2 * RING)])


def partner(level, value, beside=None, operands=()):
    def branch(level, value, *operands):
        pairs = [(r, r ^ (2**level)) for r in range(lax.axis_size("replica"))]
        got = jax.tree.map(lambda part: lax.ppermute(part, "replica", pairs), value)
        return got if beside is None else (got, beside(*operands))

    return lax.switch(level, [functools.partial(branch, k) for k in range(4)], value, *operands)


def column(place, own, shift):
    half = place[1] if own else 1 - place[1]
    block = half * RING + lax.rem(place[0] + shift, RING)
    return pl.multiple_of(block * BLOCK, BLOCK)


def call(kernel, grid, in_specs, out_specs, out_shape, flops, moved, place, *operands, after=()):
    def body(place, *refs):
        kernel(place, *refs[len(after) :])

    whole = pl.BlockSpec(memory_space=pl.ANY)
    return pl.pallas_call(
        body,
        grid_spec=pltpu.PrefetchScalarGridSpec(
            num_scalar_prefetch=1,
            grid=grid,
            in_specs=[whole] * len(after) + in_specs,
            out_specs=out_specs,
        ),
        out_shape=out_shape,
        compiler_params=pltpu.CompilerParams(vmem_limit_bytes=VMEM),
        cost_estimate=pl.CostEstimate(flops=flops, bytes_accessed=moved, transcendentals=0),
    )(place, *after, *operands)


def norm_kernel(place, hidden, gain, *outs):
    def strip(i, carry):
        here = pl.ds(pl.multiple_of(i * STRIP, STRIP), STRIP)
        rows = hidden[here, :].astype(jnp.float32)
        inverse = lax.rsqrt(jnp.mean(rows * rows, axis=-1, keepdims=True) + epsilon)
        outs[-1][here, :] = inverse
        for own in range(2):
            for shift in range(RING):
                at = pl.ds(column(place, own, shift), BLOCK)
                block = hidden[here, at].astype(jnp.float32) * inverse * gain[:, at]
                outs[own * RING + shift][here, :] = block.astype(jnp.bfloat16)
        return carry

    lax.fori_loop(0, ROWS // STRIP, strip, 0)


def norm(place, hidden, gain):
    row_block = pl.BlockSpec((ROWS, BLOCK), lambda i, p: (i, 0))
    width = hidden.shape[1]
    return call(
        norm_kernel,
        (TOK // ROWS,),
        [
            pl.BlockSpec((ROWS, width), lambda i, p: (i, 0)),
            pl.BlockSpec((1, width), lambda i, p: (0, 0)),
        ],
        [row_block] * (2 * RING) + [pl.BlockSpec((ROWS, 1), lambda i, p: (i, 0))],
        [jax.ShapeDtypeStruct((TOK, BLOCK), jnp.bfloat16)] * (2 * RING)
        + [jax.ShapeDtypeStruct((TOK, 1), jnp.float32)],
        4 * TOK * width,
        4 * TOK * width,
        place,
        hidden,
        gain,
    )


def sums_kernel(multiplier, own, place, scale, *refs):
    blocks, weighted, rest = refs[:RING], refs[RING : 2 * RING], refs[2 * RING :]
    *sends, keep = rest[own:]
    total = jnp.zeros((CUT, COLS), jnp.float32)
    for block, rows in zip(blocks, weighted):
        total += lax.dot_general(
            block[...], rows[...], (((0,), (0,)), ((), ())), preferred_element_type=jnp.float32
        )
    total = total * (scale[0, 0] * multiplier)
    if own:
        total = rest[0][...].astype(jnp.float32) - learning_rate * total
    total = total.astype(jnp.bfloat16)
    step = pl.program_id(0)
    for at, send in enumerate(sends):

        @pl.when(step == at)
        def _(send=send):
            send[...] = total

    @pl.when(step >= len(sends))
    def _():
        keep[...] = total


def sums(multiplier, own, place, scale, blocks, weighted, weight=None, after=()):
    steps = HALF // CUT

    def tile(i, p):
        return jnp.where(i < steps, 1 - p[2], p[2]) * steps + lax.rem(i, steps)

    shape = (CUT, COLS)
    extra = [pl.BlockSpec(shape, lambda i, p: (tile(i, p), 0))] if own else []
    return call(
        functools.partial(sums_kernel, multiplier, own),
        (2 * steps,),
        [pl.BlockSpec(memory_space=pltpu.SMEM)]
        + [pl.BlockSpec((TOK, CUT), lambda i, p: (0, tile(i, p)))] * RING
        + [pl.BlockSpec((TOK, COLS), lambda i, p: (0, 0))] * RING
        + extra,
        [
            *[pl.BlockSpec(shape, lambda i, p: (0, 0))] * steps,
            pl.BlockSpec(shape, lambda i, p: (jnp.maximum(i - steps, 0), 0)),
        ],
        [jax.ShapeDtypeStruct(shape, jnp.bfloat16)] * steps
        + [jax.ShapeDtypeStruct((HALF, COLS), jnp.bfloat16)],
        2 * RING * TOK * BLOCK * COLS,
        2 * 2 * RING * TOK * BLOCK + 2 * BLOCK * COLS,
        place,
        scale,
        *blocks,
        *weighted,
        *([weight] if own else []),
        after=after,
    )


def products_kernel(multiplier, place, weight, *refs):
    for rows, out in zip(refs[:RING], refs[RING:]):
        total = lax.dot_general(
            rows[...], weight[...], (((1,), (1,)), ((), ())), preferred_element_type=jnp.float32
        )
        out[...] = (multiplier * total).astype(jnp.bfloat16)


def products(multiplier, place, weight, weighted, after=()):
    width = weight.shape[0]
    return call(
        functools.partial(products_kernel, multiplier),
        (width // TILE,),
        [pl.BlockSpec((TILE, COLS), lambda i, p: (i, 0))]
        + [pl.BlockSpec((TOK, COLS), lambda i, p: (0, 0))] * RING,
        [pl.BlockSpec((TOK, TILE), lambda i, p: (0, i))] * RING,
        [jax.ShapeDtypeStruct((TOK, width), jnp.bfloat16)] * RING,
        2 * RING * TOK * width * COLS,
        2 * 2 * RING * TOK * width + 2 * width * COLS,
        place,
        weight,
        *weighted,
        after=after,
    )


def back_kernel(layout, place, scale, hidden, gain, inverse_in, *refs):
    pieces, out = refs[:-1], refs[-1]
    width = hidden.shape[1]

    def strip(i, carry):
        here = pl.ds(pl.multiple_of(i * STRIP, STRIP), STRIP)
        inverse = inverse_in[here, :]

        def parts(own, shift, offset, piece):
            start = pl.multiple_of(column(place, own, shift) + offset, TILE)
            at = pl.ds(start, piece.shape[1])
            up = piece[here, :].astype(jnp.float32) * gain[:, at]
            return at, hidden[here, at].astype(jnp.float32), up

        total = jnp.zeros((STRIP, 1), jnp.float32)
        for (own, shift, offset), piece in zip(layout, pieces):
            at, rows, up = parts(own, shift, offset, piece)
            total += jnp.sum(up * rows, axis=-1, keepdims=True)
        mean = inverse * total * (1.0 / width)
        outer = inverse * scale[0, 0]
        inner = outer * inverse * mean
        for (own, shift, offset), piece in zip(layout, pieces):
            at, rows, up = parts(own, shift, offset, piece)
            out[here, at] = (outer * up - inner * rows).astype(jnp.bfloat16)
        return carry

    lax.fori_loop(0, ROWS // STRIP, strip, 0)


def back(place, scale, hidden, gain, inverse, layout, pieces):
    width = hidden.shape[1]
    wide = pl.BlockSpec((ROWS, width), lambda i, p: (i, 0))
    return call(
        functools.partial(back_kernel, layout),
        (TOK // ROWS,),
        [
            pl.BlockSpec(memory_space=pltpu.SMEM),
            wide,
            pl.BlockSpec((1, width), lambda i, p: (0, 0)),
            pl.BlockSpec((ROWS, 1), lambda i, p: (i, 0)),
        ]
        + [pl.BlockSpec((ROWS, piece.shape[1]), lambda i, p: (i, 0)) for piece in pieces],
        wide,
        jax.ShapeDtypeStruct(hidden.shape, jnp.bfloat16),
        8 * TOK * width,
        6 * TOK * width,
        place,
        scale,
        hidden,
        gain,
        inverse,
        *pieces,
    )


def rows_kernel(place, *refs):
    for at, part in enumerate(refs[:-1]):

        @pl.when(pl.program_id(0) == at)
        def _(part=part):
            refs[-1][...] = part[...]


def rows(place, mine, theirs):
    parts = [*mine, *theirs]

    def cut(i, p):
        half = jnp.where(i < len(mine), p[2], 1 - p[2])
        return half * len(mine) + lax.rem(i, len(mine)), 0

    return call(
        rows_kernel,
        (len(parts),),
        [pl.BlockSpec((CUT, COLS), lambda i, p: (0, 0))] * len(parts),
        pl.BlockSpec((CUT, COLS), cut),
        jax.ShapeDtypeStruct((BLOCK, COLS), jnp.bfloat16),
        0,
        4 * len(parts) * CUT * COLS,
        place,
        *parts,
    )


def last_kernel(place, so_far, part, out):
    out[...] = part[...]


def last_rows(place, so_far, part):
    steps = HALF // CUT
    return pl.pallas_call(
        last_kernel,
        grid_spec=pltpu.PrefetchScalarGridSpec(
            num_scalar_prefetch=1,
            grid=(1,),
            in_specs=[
                pl.BlockSpec(memory_space=pl.ANY),
                pl.BlockSpec((CUT, COLS), lambda i, p: (0, 0)),
            ],
            out_specs=pl.BlockSpec(
                (CUT, COLS), lambda i, p: ((1 - p[2]) * steps + steps - 1, 0)
            ),
        ),
        out_shape=jax.ShapeDtypeStruct((BLOCK, COLS), jnp.bfloat16),
        input_output_aliases={1: 0},
        compiler_params=pltpu.CompilerParams(vmem_limit_bytes=VMEM),
        cost_estimate=pl.CostEstimate(flops=0, bytes_accessed=4 * CUT * COLS, transcendentals=0),
    )(place, so_far, part)


def added(kept, at, got):
    kept = kept[at * CUT : (at + 1) * CUT]
    return kept.astype(jnp.float32) + got.astype(jnp.float32)


def with_level(
    level, hidden, cotangent, weight, gain, train_logp, infer_logp, advantage, response_mask
):
    multiplier = hidden.shape[1] ** (-0.5)
    tok_replica = TOK * lax.axis_size("shard")
    shard = lax.axis_index("shard")
    bit = (lax.axis_index("replica") >> level) & 1
    place = jnp.stack([shard % RING, shard // RING, bit]).astype(jnp.int32)

    mask_f = response_mask.astype(jnp.float32)
    count = jnp.sum(mask_f)
    coefficient = mask_f * jnp.minimum(jnp.exp(train_logp - infer_logp), ratio_cap) * advantage
    weighted = (coefficient[:, None] * cotangent.astype(jnp.float32)).astype(jnp.bfloat16)
    count = jnp.broadcast_to(count.astype(jnp.bfloat16), (PAD, 128))
    pair = (count[:, :1], across(count)[:, :1])
    left = lax.broadcasted_iota(jnp.int32, (PAD, COLS), 1) < COLS // 2
    weighted = jnp.concatenate([weighted, jnp.where(left, *pair)], axis=0)

    gathered = [weighted] + [around(weighted, shift) for shift in range(1, RING)]
    far_weight = across(weight)

    *blocks, inverse = norm(place, hidden, gain)
    far_blocks = [blocks[0]] + [around(blocks[s], s) for s in range(1, RING)]
    own_blocks = [blocks[RING]] + [around(blocks[RING + s], s) for s in range(1, RING)]

    counts = sum(rows[TOK : TOK + 1].astype(jnp.float32) for rows in gathered)
    scale = tok_replica / (counts[:, :1] + counts[:, COLS // 2 : COLS // 2 + 1])

    near = products(multiplier, place, weight, gathered, after=[inverse])
    near = [near[0]] + [around(near[s], -s) for s in range(1, RING)]

    *far_send, far_keep = sums(
        multiplier, 0, place, scale, far_blocks, gathered, after=[near[0]]
    )
    far_got = partner(level, far_send)
    far_sum = [added(far_keep, at, got).astype(jnp.bfloat16) for at, got in enumerate(far_got)]
    far_sum[1], _ = lax.optimization_barrier((far_sum[1], far_weight))
    crossed = [across(part) for part in far_sum]

    *own_send, own_keep = sums(
        multiplier, 1, place, scale, own_blocks, gathered, weight, after=[far_got[0]]
    )
    own_send, _ = lax.optimization_barrier((own_send, near[1]))
    own_got = partner(level, own_send)

    far = products(multiplier, place, far_weight, gathered, after=[own_got[0], near[2]])
    far = [far[0]] + [around(far[s], -s) for s in range(1, RING)]

    def averaged(at, crossed):
        total = added(own_keep, at, own_got[at]) - learning_rate * crossed.astype(jnp.float32)
        return (total * 0.5).astype(jnp.bfloat16)

    def last(mine, theirs, scale, hidden, gain, inverse, *pieces):
        layout = [(own, s, 0) for own in range(2) for s in range(RING)]
        back_rows = back(place, scale, hidden, gain, inverse, layout, pieces)
        return back_rows, rows(place, mine, theirs)

    first, *_ = lax.optimization_barrier((averaged(0, crossed[0]), far[1], far[2]))
    theirs = [partner(level, first)]
    second, _ = lax.optimization_barrier((crossed[1], theirs[0]))
    mine = [first, averaged(1, second)]
    got, (grad_hidden, so_far) = partner(
        level, mine[1], last, (mine, theirs, scale, hidden, gain, inverse, *far, *near)
    )
    return grad_hidden, last_rows(place, so_far, got)


def on_device(
    hidden, cotangent, weight, gain, train_logp, infer_logp, advantage, response_mask, step
):
    grad_hidden, new_weight = with_level(
        step[0] % 4,
        hidden,
        cotangent,
        weight[0],
        gain[None],
        train_logp,
        infer_logp,
        advantage,
        response_mask,
    )
    return grad_hidden, new_weight[None]


def solution(mesh):
    return jax.shard_map(
        on_device,
        mesh=mesh,
        in_specs=(
            P(("replica", "shard"), None),
            P(("replica", "shard"), None),
            P("replica", "shard", None),
            P(),
            P(("replica", "shard")),
            P(("replica", "shard")),
            P(("replica", "shard")),
            P(("replica", "shard")),
            P(),
        ),
        out_specs=(P(("replica", "shard"), None), P("replica", "shard", None)),
        check_vma=False,
    )
```

```python
import functools

import jax
import jax.numpy as jnp
from jax import lax
from jax.experimental import pallas as pl
from jax.experimental.pallas import tpu as pltpu
from jax.sharding import PartitionSpec as P

ratio_cap = 2.0
epsilon = 1e-05
learning_rate = 1.0

RING = 4
BLOCK = 1024
TOK = 256
COLS = 1024
PAD = 16
ROWS = 64
STRIP = 32
HALF = BLOCK // 2
CUT = 256
TILE = 256
VMEM = 32 * 1024 * 1024


def around(value, shift):
    pairs = [(s, s // RING * RING + (s + shift) % RING) for s in range(2 * RING)]
    return lax.ppermute(value, "shard", pairs)


def across(value):
    return lax.ppermute(value, "shard", [(s, s ^ RING) for s in range(2 * RING)])


def partner(level, value, beside=None, operands=()):
    def branch(level, value, *operands):
        pairs = [(r, r ^ (2**level)) for r in range(lax.axis_size("replica"))]
        got = lax.ppermute(value, "replica", pairs)
        return got if beside is None else (got, beside(*operands))

    return lax.switch(level, [functools.partial(branch, k) for k in range(4)], value, *operands)


def column(place, own, shift):
    half = place[1] if own else 1 - place[1]
    block = half * RING + lax.rem(place[0] + shift, RING)
    return pl.multiple_of(block * BLOCK, BLOCK)


def call(kernel, grid, in_specs, out_specs, out_shape, flops, moved, place, *operands, after=()):
    def body(place, *refs):
        kernel(place, *refs[len(after) :])

    whole = pl.BlockSpec(memory_space=pl.ANY)
    return pl.pallas_call(
        body,
        grid_spec=pltpu.PrefetchScalarGridSpec(
            num_scalar_prefetch=1,
            grid=grid,
            in_specs=[whole] * len(after) + in_specs,
            out_specs=out_specs,
        ),
        out_shape=out_shape,
        compiler_params=pltpu.CompilerParams(vmem_limit_bytes=VMEM),
        cost_estimate=pl.CostEstimate(flops=flops, bytes_accessed=moved, transcendentals=0),
    )(place, *after, *operands)


def norm_kernel(place, hidden, gain, counts, *outs):
    def strip(i, carry):
        here = pl.ds(pl.multiple_of(i * STRIP, STRIP), STRIP)
        rows = hidden[here, :].astype(jnp.float32)
        inverse = lax.rsqrt(jnp.mean(rows * rows, axis=-1, keepdims=True) + epsilon)
        outs[-1][here, :] = inverse
        for own in range(2):
            for shift in range(RING):
                at = pl.ds(column(place, own, shift), BLOCK)
                block = hidden[here, at].astype(jnp.float32) * inverse * gain[:, at]
                outs[own * RING + shift][here, :] = block.astype(jnp.bfloat16)
        return carry

    last = pl.program_id(0) == TOK // ROWS

    @pl.when(jnp.logical_not(last))
    def _():
        lax.fori_loop(0, ROWS // STRIP, strip, 0)

    @pl.when(last)
    def _():
        for out in outs[:RING]:
            out[:PAD, :] = counts[...]


def norm(place, hidden, gain, counts):
    width = hidden.shape[1]
    steps = TOK // ROWS

    def clipped(i, p):
        return jnp.minimum(i, steps - 1), 0

    return call(
        norm_kernel,
        (steps + 1,),
        [
            pl.BlockSpec((ROWS, width), clipped),
            pl.BlockSpec((1, width), lambda i, p: (0, 0)),
            pl.BlockSpec((PAD, BLOCK), lambda i, p: (0, 0)),
        ],
        [pl.BlockSpec((ROWS, BLOCK), lambda i, p: (i, 0))] * RING
        + [pl.BlockSpec((ROWS, BLOCK), clipped)] * RING
        + [pl.BlockSpec((ROWS, 1), clipped)],
        [jax.ShapeDtypeStruct((TOK + PAD, BLOCK), jnp.bfloat16)] * RING
        + [jax.ShapeDtypeStruct((2 * TOK, BLOCK), jnp.bfloat16)] * RING
        + [jax.ShapeDtypeStruct((TOK, 1), jnp.float32)],
        4 * TOK * width,
        4 * TOK * width,
        place,
        hidden,
        gain,
        counts,
    )


def sums_kernel(multiplier, own, place, scale, *refs):
    blocks, weighted, rest = refs[:RING], refs[RING : 2 * RING], refs[2 * RING :]
    *sends, keep = rest[own:]
    total = jnp.zeros((CUT, COLS), jnp.float32)
    for block, rows in zip(blocks, weighted):
        total += lax.dot_general(
            block[...], rows[...], (((0,), (0,)), ((), ())), preferred_element_type=jnp.float32
        )
    total = total * (scale[0, 0] * multiplier)
    if own:
        total = rest[0][...].astype(jnp.float32) - learning_rate * total
    total = total.astype(jnp.bfloat16)
    step = pl.program_id(0)
    for at in range(HALF // CUT):

        @pl.when(step == at)
        def _(at=at):
            sends[min(at, len(sends) - 1)][...] = total

    @pl.when(step >= HALF // CUT)
    def _():
        keep[...] = total


def sums(multiplier, own, place, scale, blocks, weighted, weight=None, after=()):
    steps = HALF // CUT
    sends = steps if own else 1

    def tile(i, p):
        return jnp.where(i < steps, 1 - p[2], p[2]) * steps + lax.rem(i, steps)

    shape = (CUT, COLS)
    extra = [pl.BlockSpec(shape, lambda i, p: (tile(i, p), 0))] if own else []
    return call(
        functools.partial(sums_kernel, multiplier, own),
        (2 * steps,),
        [pl.BlockSpec(memory_space=pltpu.SMEM)]
        + [pl.BlockSpec((TOK, CUT), lambda i, p: (0, tile(i, p)))] * RING
        + [pl.BlockSpec((TOK, COLS), lambda i, p: (0, 0))] * RING
        + extra,
        [
            *[pl.BlockSpec(shape, lambda i, p: (jnp.minimum(i, steps // sends - 1), 0))] * sends,
            pl.BlockSpec(shape, lambda i, p: (jnp.maximum(i - steps, 0), 0)),
        ],
        [jax.ShapeDtypeStruct((HALF // sends, COLS), jnp.bfloat16)] * sends
        + [jax.ShapeDtypeStruct((HALF, COLS), jnp.bfloat16)],
        2 * RING * TOK * BLOCK * COLS,
        2 * 2 * RING * TOK * BLOCK + 2 * BLOCK * COLS,
        place,
        scale,
        *blocks,
        *weighted,
        *([weight] if own else []),
        after=after,
    )


def products_kernel(multiplier, place, gain, weight, *refs):
    factor = multiplier * gain[...]
    for rows, out in zip(refs[:RING], refs[RING:]):
        total = lax.dot_general(
            rows[...], weight[...], (((1,), (1,)), ((), ())), preferred_element_type=jnp.float32
        )
        out[...] = (factor * total).astype(jnp.bfloat16)


def products(multiplier, place, own, gain, weight, weighted, below=(), after=()):
    def gain_at(i, p):
        half = p[1] if own else 1 - p[1]
        return 0, (half * RING + p[0]) * (BLOCK // CUT) + i

    kept = len(after)

    def body(place, *refs):
        products_kernel(multiplier, place, *refs[kept + len(below) :])

    whole = pl.BlockSpec(memory_space=pl.ANY)
    rows = 2 * TOK if below else TOK
    return pl.pallas_call(
        body,
        grid_spec=pltpu.PrefetchScalarGridSpec(
            num_scalar_prefetch=1,
            grid=(BLOCK // CUT,),
            in_specs=[whole] * (kept + len(below))
            + [pl.BlockSpec((1, CUT), gain_at), pl.BlockSpec((CUT, COLS), lambda i, p: (i, 0))]
            + [pl.BlockSpec((TOK, COLS), lambda i, p: (0, 0))] * RING,
            out_specs=[pl.BlockSpec((TOK, CUT), lambda i, p: (rows // TOK - 1, i))] * RING,
        ),
        out_shape=[jax.ShapeDtypeStruct((rows, BLOCK), jnp.bfloat16)] * RING,
        input_output_aliases={1 + kept + at: at for at in range(len(below))},
        compiler_params=pltpu.CompilerParams(vmem_limit_bytes=VMEM),
        cost_estimate=pl.CostEstimate(
            flops=2 * RING * TOK * BLOCK * COLS,
            bytes_accessed=2 * 2 * RING * TOK * BLOCK + 2 * BLOCK * COLS,
            transcendentals=0,
        ),
    )(place, *after, *below, gain, weight, *weighted)


def back_kernel(place, scale, hidden, inverse_in, *refs):
    pieces, out = refs[:-1], refs[-1]
    width = hidden.shape[1]

    def strip(i, carry):
        here = pl.ds(pl.multiple_of(i * STRIP, STRIP), STRIP)
        inverse = inverse_in[here, :]

        def parts(at, piece):
            columns = pl.ds(column(place, at // RING, at % RING), BLOCK)
            rows = hidden[here, columns].astype(jnp.float32)
            return columns, rows, piece[here, :].astype(jnp.float32)

        total = jnp.zeros((STRIP, BLOCK), jnp.float32)
        for at, piece in enumerate(pieces):
            _, rows, up = parts(at, piece)
            total += up * rows
        mean = inverse * jnp.sum(total, axis=-1, keepdims=True) * (1.0 / width)
        outer = inverse * scale[0, 0]
        inner = outer * inverse * mean
        for at, piece in enumerate(pieces):
            columns, rows, up = parts(at, piece)
            out[here, columns] = (outer * up - inner * rows).astype(jnp.bfloat16)
        return carry

    lax.fori_loop(0, ROWS // STRIP, strip, 0)


def back(place, scale, hidden, inverse, pieces):
    width = hidden.shape[1]
    wide = pl.BlockSpec((ROWS, width), lambda i, p: (i, 0))
    return call(
        back_kernel,
        (TOK // ROWS,),
        [
            pl.BlockSpec(memory_space=pltpu.SMEM),
            wide,
            pl.BlockSpec((ROWS, 1), lambda i, p: (i, 0)),
        ]
        + [
            pl.BlockSpec((ROWS, BLOCK), lambda i, p, at=piece.shape[0] // TOK - 1: (at * TOK // ROWS + i, 0))
            for piece in pieces
        ],
        wide,
        pltpu.HBM(hidden.shape, jnp.bfloat16),
        6 * TOK * width,
        6 * TOK * width,
        place,
        scale,
        hidden,
        inverse,
        *pieces,
    )


def rows_kernel(place, *refs):
    for at, part in enumerate(refs[:-1]):

        @pl.when(pl.program_id(0) == at)
        def _(part=part):
            refs[-1][...] = part[...]


def rows(place, mine, theirs):
    parts = [*mine, *theirs]

    def cut(i, p):
        half = jnp.where(i < len(mine), p[2], 1 - p[2])
        return half * len(mine) + lax.rem(i, len(mine)), 0

    return call(
        rows_kernel,
        (len(parts),),
        [pl.BlockSpec((CUT, COLS), lambda i, p: (0, 0))] * len(parts),
        pl.BlockSpec((CUT, COLS), cut),
        pltpu.HBM((BLOCK, COLS), jnp.bfloat16),
        0,
        4 * len(parts) * CUT * COLS,
        place,
        *parts,
    )


def last_kernel(place, so_far, part, out):
    out[...] = part[...]


def last_rows(place, so_far, part):
    steps = HALF // CUT
    return pl.pallas_call(
        last_kernel,
        grid_spec=pltpu.PrefetchScalarGridSpec(
            num_scalar_prefetch=1,
            grid=(1,),
            in_specs=[
                pl.BlockSpec(memory_space=pltpu.HBM),
                pl.BlockSpec((CUT, COLS), lambda i, p: (0, 0)),
            ],
            out_specs=pl.BlockSpec(
                (CUT, COLS), lambda i, p: ((1 - p[2]) * steps + steps - 1, 0)
            ),
        ),
        out_shape=pltpu.HBM((BLOCK, COLS), jnp.bfloat16),
        input_output_aliases={1: 0},
        compiler_params=pltpu.CompilerParams(vmem_limit_bytes=VMEM),
        cost_estimate=pl.CostEstimate(flops=0, bytes_accessed=4 * CUT * COLS, transcendentals=0),
    )(place, so_far, part)


def added(kept, got, at):
    return kept[at * CUT : (at + 1) * CUT].astype(jnp.float32) + got.astype(jnp.float32)


def with_level(
    level, hidden, cotangent, weight, gain, train_logp, infer_logp, advantage, response_mask
):
    multiplier = hidden.shape[1] ** (-0.5)
    tok_replica = TOK * lax.axis_size("shard")
    shard = lax.axis_index("shard")
    bit = (lax.axis_index("replica") >> level) & 1
    place = jnp.stack([shard % RING, shard // RING, bit]).astype(jnp.int32)

    mask_f = response_mask.astype(jnp.float32)
    count = jnp.sum(mask_f)
    coefficient = mask_f * jnp.minimum(jnp.exp(train_logp - infer_logp), ratio_cap) * advantage
    weighted = (coefficient[:, None] * cotangent.astype(jnp.float32)).astype(jnp.bfloat16)
    gathered = [weighted] + [around(weighted, shift) for shift in range(1, RING)]
    count = jnp.broadcast_to(count.astype(jnp.bfloat16), (PAD, 128))
    count, _ = lax.optimization_barrier((count, weighted))
    pair = (count[:, :1], across(count)[:, :1])
    left = lax.broadcasted_iota(jnp.int32, (PAD, BLOCK), 1) < BLOCK // 2
    counts = jnp.where(left, *pair)
    far_weight = across(weight)

    *blocks, inverse = norm(place, hidden, gain, counts)
    far_blocks = [blocks[0]] + [around(blocks[s], s) for s in range(1, RING)]
    counts = sum(rows[TOK : TOK + 1].astype(jnp.float32) for rows in far_blocks)
    scale = tok_replica / (counts[:, :1] + counts[:, BLOCK // 2 : BLOCK // 2 + 1])

    below = [blocks[RING]] + [blocks[2 * RING - s] for s in range(1, RING)]
    both = products(multiplier, place, 1, gain, weight, gathered, below, after=[inverse])
    both = [both[0]] + [around(both[RING - s], s) for s in range(1, RING)]
    near = [both[0]] + [both[RING - s] for s in range(1, RING)]

    far_send, far_keep = sums(
        multiplier, 0, place, scale, far_blocks, gathered, after=[both[0]]
    )
    far_got = partner(level, far_send)
    far_sum = [
        added(far_keep, far_got[at * CUT : (at + 1) * CUT], at).astype(jnp.bfloat16)
        for at in range(HALF // CUT)
    ]
    far_sum[1], _ = lax.optimization_barrier((far_sum[1], far_weight))
    crossed = [across(part) for part in far_sum]

    *own_send, own_keep = sums(
        multiplier, 1, place, scale, both, gathered, weight, after=[far_got]
    )
    def meanwhile(gain, far_weight, *gathered):
        return products(multiplier, place, 0, gain, far_weight, gathered)

    got, far = partner(level, own_send[0], meanwhile, (gain, far_weight, *gathered))
    own_got = [got]
    second, _ = lax.optimization_barrier((own_send[1], far[0]))
    far = [far[0]] + [around(far[s], -s) for s in range(1, RING)]
    own_got.append(partner(level, second))

    def averaged(at, crossed):
        total = added(own_keep, own_got[at], at) - learning_rate * crossed.astype(jnp.float32)
        return (total * 0.5).astype(jnp.bfloat16)

    def last(mine, theirs, scale, hidden, inverse, *pieces):
        back_rows = back(place, scale, hidden, inverse, pieces)
        return back_rows, rows(place, mine, theirs)

    first, *_ = lax.optimization_barrier((averaged(0, crossed[0]), own_got[1], far[1], far[2]))
    theirs = [partner(level, first)]
    second, _ = lax.optimization_barrier((crossed[1], theirs[0]))
    mine = [first, averaged(1, second)]
    got, (grad_hidden, so_far) = partner(
        level, mine[1], last, (mine, theirs, scale, hidden, inverse, *far, *near)
    )
    return grad_hidden, last_rows(place, so_far, got)


def on_device(
    hidden, cotangent, weight, gain, train_logp, infer_logp, advantage, response_mask, step
):
    grad_hidden, new_weight = with_level(
        step[0] % 4,
        hidden,
        cotangent,
        weight[0],
        gain[None],
        train_logp,
        infer_logp,
        advantage,
        response_mask,
    )
    return grad_hidden, new_weight[None]


def solution(mesh):
    return jax.shard_map(
        on_device,
        mesh=mesh,
        in_specs=(
            P(("replica", "shard"), None),
            P(("replica", "shard"), None),
            P("replica", "shard", None),
            P(),
            P(("replica", "shard")),
            P(("replica", "shard")),
            P(("replica", "shard")),
            P(("replica", "shard")),
            P(),
        ),
        out_specs=(P(("replica", "shard"), None), P("replica", "shard", None)),
        check_vma=False,
    )
```

```python
import functools

import jax
import jax.numpy as jnp
from jax import lax
from jax.experimental import pallas as pl
from jax.experimental.pallas import tpu as pltpu
from jax.sharding import PartitionSpec as P

ratio_cap = 2.0
epsilon = 1e-05
learning_rate = 1.0

RING = 4
BLOCK = 1024
TOK = 256
COLS = 1024
PAD = 16
ROWS = 64
STRIP = 32
HALF = BLOCK // 2
CUT = 256
TILE = 256
VMEM = 32 * 1024 * 1024


def around(value, shift):
    pairs = [(s, s // RING * RING + (s + shift) % RING) for s in range(2 * RING)]
    return lax.ppermute(value, "shard", pairs)


def across(value):
    return lax.ppermute(value, "shard", [(s, s ^ RING) for s in range(2 * RING)])


def partner(level, value, beside=None, operands=()):
    def branch(level, value, *operands):
        pairs = [(r, r ^ (2**level)) for r in range(lax.axis_size("replica"))]
        got = lax.ppermute(value, "replica", pairs)
        return got if beside is None else (got, beside(*operands))

    return lax.switch(level, [functools.partial(branch, k) for k in range(4)], value, *operands)


def column(place, own, shift):
    half = place[1] if own else 1 - place[1]
    block = half * RING + lax.rem(place[0] + shift, RING)
    return pl.multiple_of(block * BLOCK, BLOCK)


def call(kernel, grid, in_specs, out_specs, out_shape, flops, moved, place, *operands, after=()):
    def body(place, *refs):
        kernel(place, *refs[len(after) :])

    whole = pl.BlockSpec(memory_space=pl.ANY)
    return pl.pallas_call(
        body,
        grid_spec=pltpu.PrefetchScalarGridSpec(
            num_scalar_prefetch=1,
            grid=grid,
            in_specs=[whole] * len(after) + in_specs,
            out_specs=out_specs,
        ),
        out_shape=out_shape,
        compiler_params=pltpu.CompilerParams(vmem_limit_bytes=VMEM),
        cost_estimate=pl.CostEstimate(flops=flops, bytes_accessed=moved, transcendentals=0),
    )(place, *after, *operands)


def norm_kernel(place, hidden, gain, counts, *outs):
    def strip(i, carry):
        here = pl.ds(pl.multiple_of(i * STRIP, STRIP), STRIP)
        rows = hidden[here, :].astype(jnp.float32)
        inverse = lax.rsqrt(jnp.mean(rows * rows, axis=-1, keepdims=True) + epsilon)
        outs[-1][here, :] = inverse
        for own in range(2):
            for shift in range(RING):
                at = pl.ds(column(place, own, shift), BLOCK)
                block = hidden[here, at].astype(jnp.float32) * inverse * gain[:, at]
                outs[own * RING + shift][here, :] = block.astype(jnp.bfloat16)
        return carry

    last = pl.program_id(0) == TOK // ROWS

    @pl.when(jnp.logical_not(last))
    def _():
        lax.fori_loop(0, ROWS // STRIP, strip, 0)

    @pl.when(last)
    def _():
        for out in outs[:RING]:
            out[:PAD, :] = counts[...]


def norm(place, hidden, gain, counts):
    width = hidden.shape[1]
    steps = TOK // ROWS

    def clipped(i, p):
        return jnp.minimum(i, steps - 1), 0

    return call(
        norm_kernel,
        (steps + 1,),
        [
            pl.BlockSpec((ROWS, width), clipped),
            pl.BlockSpec((1, width), lambda i, p: (0, 0)),
            pl.BlockSpec((PAD, BLOCK), lambda i, p: (0, 0)),
        ],
        [pl.BlockSpec((ROWS, BLOCK), lambda i, p: (i, 0))] * RING
        + [pl.BlockSpec((ROWS, BLOCK), clipped)] * RING
        + [pl.BlockSpec((ROWS, 1), clipped)],
        [jax.ShapeDtypeStruct((TOK + PAD, BLOCK), jnp.bfloat16)] * RING
        + [jax.ShapeDtypeStruct((2 * TOK, BLOCK), jnp.bfloat16)] * RING
        + [jax.ShapeDtypeStruct((TOK, 1), jnp.float32)],
        4 * TOK * width,
        4 * TOK * width,
        place,
        hidden,
        gain,
        counts,
    )


def sums_kernel(multiplier, tokens, own, place, *refs):
    blocks, weighted = refs[:RING], refs[RING : 2 * RING]
    rest, (left, right) = refs[2 * RING : -2], refs[-2:]
    step = pl.program_id(0)

    @pl.when(step == 0)
    def _():
        for at, rows in enumerate(weighted):
            right[at * TOK : (at + 1) * TOK, :] = rows[...]

    for at, block in enumerate(blocks):
        left[at * TOK : (at + 1) * TOK, :] = block[...]
    total = lax.dot_general(
        left[...], right[...], (((0,), (0,)), ((), ())), preferred_element_type=jnp.float32
    )
    if own:
        scale_in, weight, *sends, keep = rest
        scale = scale_in[:1, :1]
        total = weight[...].astype(jnp.float32) - learning_rate * (total * (scale * multiplier))
    else:
        *counts, send, keep, scale_out = rest
        sends = [send]
        count = sum(part[:1, :].astype(jnp.float32) for part in counts)
        scale = tokens / (count[:, :1] + count[:, BLOCK // 2 : BLOCK // 2 + 1])
        scale_out[...] = jnp.broadcast_to(scale, scale_out.shape)
        total = total * (scale * multiplier)
    total = total.astype(jnp.bfloat16)
    for at in range(HALF // CUT):

        @pl.when(step == at)
        def _(at=at):
            sends[min(at, len(sends) - 1)][...] = total

    @pl.when(step >= HALF // CUT)
    def _():
        keep[...] = total


def sums(multiplier, tokens, own, place, blocks, weighted, scale=None, weight=None, after=()):
    steps = HALF // CUT
    sends = steps if own else 1
    kept = len(after)

    def tile(i, p):
        return jnp.where(i < steps, 1 - p[2], p[2]) * steps + lax.rem(i, steps)

    def body(place, *refs):
        sums_kernel(multiplier, tokens, own, place, *refs[kept:])

    shape = (CUT, COLS)
    flat = pl.BlockSpec((8, 128), lambda i, p: (0, 0))
    if own:
        extra, more = [flat, pl.BlockSpec(shape, lambda i, p: (tile(i, p), 0))], [scale, weight]
    else:
        extra, more = [pl.BlockSpec((PAD, BLOCK), lambda i, p: (TOK // PAD, 0))] * RING, blocks
    return pl.pallas_call(
        body,
        grid_spec=pltpu.PrefetchScalarGridSpec(
            num_scalar_prefetch=1,
            grid=(2 * steps,),
            in_specs=[pl.BlockSpec(memory_space=pl.ANY)] * kept
            + [pl.BlockSpec((TOK, CUT), lambda i, p: (0, tile(i, p)))] * RING
            + [pl.BlockSpec((TOK, COLS), lambda i, p: (0, 0))] * RING
            + extra,
            out_specs=[pl.BlockSpec(shape, lambda i, p: (jnp.minimum(i, steps // sends - 1), 0))]
            * sends
            + [pl.BlockSpec(shape, lambda i, p: (jnp.maximum(i - steps, 0), 0))]
            + ([] if own else [flat]),
            scratch_shapes=[
                pltpu.VMEM((RING * TOK, CUT), jnp.bfloat16),
                pltpu.VMEM((RING * TOK, COLS), jnp.bfloat16),
            ],
        ),
        out_shape=[jax.ShapeDtypeStruct((HALF // sends, COLS), jnp.bfloat16)] * sends
        + [jax.ShapeDtypeStruct((HALF, COLS), jnp.bfloat16)]
        + ([] if own else [jax.ShapeDtypeStruct((8, 128), jnp.float32)]),
        compiler_params=pltpu.CompilerParams(vmem_limit_bytes=VMEM),
        cost_estimate=pl.CostEstimate(
            flops=2 * RING * TOK * BLOCK * COLS,
            bytes_accessed=2 * 2 * RING * TOK * BLOCK + 2 * BLOCK * COLS,
            transcendentals=0,
        ),
    )(place, *after, *blocks, *weighted, *more)


def products_kernel(multiplier, place, gain, weight, *refs):
    factor = multiplier * gain[...]
    for rows, out in zip(refs[:RING], refs[RING:]):
        total = lax.dot_general(
            rows[...], weight[...], (((1,), (1,)), ((), ())), preferred_element_type=jnp.float32
        )
        out[...] = (factor * total).astype(jnp.bfloat16)


def products(multiplier, place, own, gain, weight, weighted, below=(), after=()):
    def gain_at(i, p):
        half = p[1] if own else 1 - p[1]
        return 0, (half * RING + p[0]) * (BLOCK // CUT) + i

    kept = len(after)

    def body(place, *refs):
        products_kernel(multiplier, place, *refs[kept + len(below) :])

    whole = pl.BlockSpec(memory_space=pl.ANY)
    rows = 2 * TOK if below else TOK
    return pl.pallas_call(
        body,
        grid_spec=pltpu.PrefetchScalarGridSpec(
            num_scalar_prefetch=1,
            grid=(BLOCK // CUT,),
            in_specs=[whole] * (kept + len(below))
            + [pl.BlockSpec((1, CUT), gain_at), pl.BlockSpec((CUT, COLS), lambda i, p: (i, 0))]
            + [pl.BlockSpec((TOK, COLS), lambda i, p: (0, 0))] * RING,
            out_specs=[pl.BlockSpec((TOK, CUT), lambda i, p: (rows // TOK - 1, i))] * RING,
        ),
        out_shape=[jax.ShapeDtypeStruct((rows, BLOCK), jnp.bfloat16)] * RING,
        input_output_aliases={1 + kept + at: at for at in range(len(below))},
        compiler_params=pltpu.CompilerParams(vmem_limit_bytes=VMEM),
        cost_estimate=pl.CostEstimate(
            flops=2 * RING * TOK * BLOCK * COLS,
            bytes_accessed=2 * 2 * RING * TOK * BLOCK + 2 * BLOCK * COLS,
            transcendentals=0,
        ),
    )(place, *after, *below, gain, weight, *weighted)


def back_kernel(place, scale, hidden, inverse_in, *refs):
    pieces, out = refs[:-1], refs[-1]
    width = hidden.shape[1]

    def strip(i, carry):
        here = pl.ds(pl.multiple_of(i * STRIP, STRIP), STRIP)
        inverse = inverse_in[here, :]

        def parts(at, piece):
            columns = pl.ds(column(place, at // RING, at % RING), BLOCK)
            rows = hidden[here, columns].astype(jnp.float32)
            return columns, rows, piece[here, :].astype(jnp.float32)

        total = jnp.zeros((STRIP, BLOCK), jnp.float32)
        for at, piece in enumerate(pieces):
            _, rows, up = parts(at, piece)
            total += up * rows
        mean = inverse * jnp.sum(total, axis=-1, keepdims=True) * (1.0 / width)
        outer = inverse * scale[:1, :1]
        inner = outer * inverse * mean
        for at, piece in enumerate(pieces):
            columns, rows, up = parts(at, piece)
            out[here, columns] = (outer * up - inner * rows).astype(jnp.bfloat16)
        return carry

    lax.fori_loop(0, ROWS // STRIP, strip, 0)


def back(place, scale, hidden, inverse, pieces):
    width = hidden.shape[1]
    wide = pl.BlockSpec((ROWS, width), lambda i, p: (i, 0))
    return call(
        back_kernel,
        (TOK // ROWS,),
        [
            pl.BlockSpec((8, 128), lambda i, p: (0, 0)),
            wide,
            pl.BlockSpec((ROWS, 1), lambda i, p: (i, 0)),
        ]
        + [
            pl.BlockSpec((ROWS, BLOCK), lambda i, p, at=piece.shape[0] // TOK - 1: (at * TOK // ROWS + i, 0))
            for piece in pieces
        ],
        wide,
        pltpu.HBM(hidden.shape, jnp.bfloat16),
        6 * TOK * width,
        6 * TOK * width,
        place,
        scale,
        hidden,
        inverse,
        *pieces,
    )


def rows_kernel(place, *refs):
    for at, part in enumerate(refs[:-1]):

        @pl.when(pl.program_id(0) // 2 == at)
        def _(part=part):
            refs[-1][...] = part[...]


def rows(place, mine, theirs):
    parts = [*mine, *theirs]
    shape = (CUT // 2, COLS)

    def cut(i, p):
        half = jnp.where(i < 2 * len(mine), p[2], 1 - p[2])
        return half * 2 * len(mine) + lax.rem(i, 2 * len(mine)), 0

    return call(
        rows_kernel,
        (2 * len(parts),),
        [
            pl.BlockSpec(shape, lambda i, p, at=at: (jnp.clip(i - 2 * at, 0, 1), 0))
            for at in range(len(parts))
        ],
        pl.BlockSpec(shape, cut),
        pltpu.HBM((BLOCK, COLS), jnp.bfloat16),
        0,
        4 * len(parts) * CUT * COLS,
        place,
        *parts,
    )


def last_kernel(place, so_far, part, out):
    out[...] = part[...]


def last_rows(place, so_far, part):
    steps = HALF // CUT
    return pl.pallas_call(
        last_kernel,
        grid_spec=pltpu.PrefetchScalarGridSpec(
            num_scalar_prefetch=1,
            grid=(2,),
            in_specs=[
                pl.BlockSpec(memory_space=pltpu.HBM),
                pl.BlockSpec((CUT // 2, COLS), lambda i, p: (i, 0)),
            ],
            out_specs=pl.BlockSpec(
                (CUT // 2, COLS), lambda i, p: (2 * ((1 - p[2]) * steps + steps - 1) + i, 0)
            ),
        ),
        out_shape=pltpu.HBM((BLOCK, COLS), jnp.bfloat16),
        input_output_aliases={1: 0},
        compiler_params=pltpu.CompilerParams(vmem_limit_bytes=VMEM),
        cost_estimate=pl.CostEstimate(flops=0, bytes_accessed=4 * CUT * COLS, transcendentals=0),
    )(place, so_far, part)


def added(kept, got, at):
    return kept[at * CUT : (at + 1) * CUT].astype(jnp.float32) + got.astype(jnp.float32)


def with_level(
    level, hidden, cotangent, weight, gain, train_logp, infer_logp, advantage, response_mask
):
    multiplier = hidden.shape[1] ** (-0.5)
    tok_replica = TOK * lax.axis_size("shard")
    shard = lax.axis_index("shard")
    bit = (lax.axis_index("replica") >> level) & 1
    place = jnp.stack([shard % RING, shard // RING, bit]).astype(jnp.int32)

    mask_f = response_mask.astype(jnp.float32)
    count = jnp.sum(mask_f)
    coefficient = mask_f * jnp.minimum(jnp.exp(train_logp - infer_logp), ratio_cap) * advantage
    weighted = (coefficient[:, None] * cotangent.astype(jnp.float32)).astype(jnp.bfloat16)
    gathered = [weighted] + [around(weighted, shift) for shift in range(1, RING)]
    count = jnp.broadcast_to(count.astype(jnp.bfloat16), (PAD, 128))
    count, _ = lax.optimization_barrier((count, weighted))
    pair = (count[:, :1], across(count)[:, :1])
    left = lax.broadcasted_iota(jnp.int32, (PAD, BLOCK), 1) < BLOCK // 2
    counts = jnp.where(left, *pair)
    far_weight = across(weight)

    *blocks, inverse = norm(place, hidden, gain, counts)
    far_blocks = [blocks[0]] + [around(blocks[s], s) for s in range(1, RING)]
    below = [blocks[RING]] + [blocks[2 * RING - s] for s in range(1, RING)]
    both = products(multiplier, place, 1, gain, weight, gathered, below, after=[inverse])
    both = [both[0]] + [around(both[RING - s], s) for s in range(1, RING)]
    near = [both[0]] + [both[RING - s] for s in range(1, RING)]

    far_send, far_keep, scale = sums(
        multiplier, tok_replica, 0, place, far_blocks, gathered, after=[both[0]]
    )
    far_got = partner(level, far_send)
    far_sum = [
        added(far_keep, far_got[at * CUT : (at + 1) * CUT], at).astype(jnp.bfloat16)
        for at in range(HALF // CUT)
    ]
    far_sum[1], _ = lax.optimization_barrier((far_sum[1], far_weight))
    crossed = [across(part) for part in far_sum]

    *own_send, own_keep = sums(
        multiplier, tok_replica, 1, place, both, gathered, scale, weight, after=[far_got]
    )
    def meanwhile(gain, far_weight, *gathered):
        return products(multiplier, place, 0, gain, far_weight, gathered)

    got, far = partner(level, own_send[0], meanwhile, (gain, far_weight, *gathered))
    own_got = [got]
    second, _ = lax.optimization_barrier((own_send[1], far[0]))
    far = [far[0]] + [around(far[s], -s) for s in range(1, RING)]
    own_got.append(partner(level, second))

    def averaged(at, crossed):
        total = added(own_keep, own_got[at], at) - learning_rate * crossed.astype(jnp.float32)
        return (total * 0.5).astype(jnp.bfloat16)

    def last(mine, theirs, scale, hidden, inverse, *pieces):
        back_rows = back(place, scale, hidden, inverse, pieces)
        return back_rows, rows(place, mine, theirs)

    first, *_ = lax.optimization_barrier((averaged(0, crossed[0]), own_got[1], far[1], far[2]))
    theirs = [partner(level, first)]
    second, _ = lax.optimization_barrier((crossed[1], theirs[0]))
    mine = [first, averaged(1, second)]
    got, (grad_hidden, so_far) = partner(
        level, mine[1], last, (mine, theirs, scale, hidden, inverse, *far, *near)
    )
    return grad_hidden, last_rows(place, so_far, got)


def on_device(
    hidden, cotangent, weight, gain, train_logp, infer_logp, advantage, response_mask, step
):
    grad_hidden, new_weight = with_level(
        step[0] % 4,
        hidden,
        cotangent,
        weight[0],
        gain[None],
        train_logp,
        infer_logp,
        advantage,
        response_mask,
    )
    return grad_hidden, new_weight[None]


def solution(mesh):
    return jax.shard_map(
        on_device,
        mesh=mesh,
        in_specs=(
            P(("replica", "shard"), None),
            P(("replica", "shard"), None),
            P("replica", "shard", None),
            P(),
            P(("replica", "shard")),
            P(("replica", "shard")),
            P(("replica", "shard")),
            P(("replica", "shard")),
            P(),
        ),
        out_specs=(P(("replica", "shard"), None), P("replica", "shard", None)),
        check_vma=False,
    )
```
